32 devices in a mesh: row: 4 (over z), col: 8 (over y, x, core).
Axes of the slice: x: 2, y: 2, z: 4, core: 2. Of those that a mesh axis runs over, the one named last changes fastest.
Arguments:
- rhs_atlas: float32 [32768, 4096], P('row', 'col'), may hold values from -6 to 6
- tile_block: int32 [64], replicated, may hold values from 0 to 63, as said below
- panels: float32 [2, 512, 32768], P(None, 'col', 'row'), may hold values from -0.1875 to 0.1875
- diag_inverse: float32 [2, 512, 512], replicated, as said below
Outputs:
- solved: float32 [2, 512, 4096], P(None, None, 'col')
- trailing: float32 [32768, 4096], P('row', 'col')
The draws below stay inside these ranges and needn't reach their ends.
Inputs may be any that keep to these rules, and one draw needn't show every extreme that they name: tile_block is a permutation of 0 to 63, and each aligned block of 16 entries holds exactly 4 entries of every residue modulo 4. `diag_inverse`: each matrix is lower triangular with diagonal entries between 0.5 and 1.5.
All inputs are finite; a program needn't handle non-finite values.
Results may differ from the reference program's by a relative error of at most 0.00008.
Values sent between devices are 32-bit elements; how exact they have to be, the bound alone decides.
No kernel may reach another device: no remote copies, remote signals or barrier semaphores. Data moves between devices by JAX's collectives and lax.ppermute only.
A program may use at most 128 MiB of HBM per device.

```python
import math
import jax
import jax.numpy as jnp
from jax import lax

NB = 512
NRHS = 4096
MB_DEV = 16
M = 32768
N_ROW = 4


def draw_tile_block(key, part):
    share = MB_DEV // N_ROW
    source_keys = jax.random.split(jax.random.fold_in(key, 11), N_ROW)
    places = jax.vmap(lambda k: jax.random.permutation(k, MB_DEV))(source_keys)
    target = places // share
    within = places % share
    target_keys = jax.random.split(jax.random.fold_in(key, 12), N_ROW)
    shuffle = jax.vmap(lambda k: jax.random.permutation(k, MB_DEV))(target_keys)
    source = jnp.arange(N_ROW, dtype=jnp.int32)[:, None]
    local_block = shuffle[target, source * share + within]
    return (local_block * N_ROW + target).reshape(-1).astype(jnp.int32)


def draw_diag_inverse(key, part):
    key_off = jax.random.fold_in(key, 21)
    key_diag = jax.random.fold_in(key, 22)
    rows = jnp.arange(NB)[:, None]
    columns = jnp.arange(NB)[None, :]
    off = jax.random.normal(key_off, (2, NB, NB), jnp.float32)
    diag = jax.random.uniform(key_diag, (2, NB), jnp.float32, 0.6, 1.4)
    below = jnp.where(columns < rows, off / math.sqrt(NB), 0.0)
    on_diag = jnp.where(columns == rows, diag[:, :, None], 0.0)
    return (below + on_diag).astype(jnp.float32)


def levels(own_key, shape, cuts, least, largest):
    factor_of = 1.0
    for position, shards_of in cuts:
        heights = jax.random.uniform(jax.random.fold_in(jax.random.fold_in(own_key, 6), position), (shards_of,), jnp.float32, least / len(cuts), largest / len(cuts))
        factor_of = factor_of * jnp.repeat(jnp.exp(heights), shape[position] // shards_of).reshape((-1,) + (1,) * (len(shape) - 1 - position))
    return factor_of


def bell_draw(own_key, extent, spread, most, cuts=(), kind=jnp.bfloat16):
    factor_of = levels(own_key, extent, cuts, -0.22, 0.18) if cuts else 1.0
    array = jax.random.normal(own_key, extent, jnp.float32) * spread * factor_of
    return jnp.minimum(jnp.maximum(array, -most), most).astype(kind)


def setup_inputs(seed: int = 0) -> dict:
    key_list = jax.random.split(jax.random.key(seed), 5)
    return {
        "rhs_atlas": bell_draw(key_list[0], (M, NRHS), 1.0, 6.0, ((0, 4), (1, 8)), jnp.float32),
        "tile_block": draw_tile_block(jax.random.fold_in(key_list[4], 71), 0),
        "panels": bell_draw(key_list[2], (2, NB, M), (2 * NB) ** -0.5, 0.1875, ((1, 8), (2, 4)), jnp.float32),
        "diag_inverse": draw_diag_inverse(jax.random.fold_in(key_list[4], 71), 0),
    }


def reference(rhs_atlas, tile_block, panels, diag_inverse):
    highest = lax.Precision.HIGHEST
    count = MB_DEV * N_ROW
    tiles = rhs_atlas.reshape(count, NB, NRHS)
    order = jnp.argsort(tile_block).astype(jnp.int32)
    rhs = jnp.take(tiles, order, axis=0)
    block_ids = jnp.arange(count, dtype=jnp.int32)
    slot = (block_ids % N_ROW) * MB_DEV + block_ids // N_ROW

    def lower(which):
        pan = panels[which].reshape(NB, count, NB)
        pan = jnp.take(pan, slot, axis=1)
        return jnp.transpose(pan, (1, 2, 0)).reshape(count * NB, NB)

    first = jnp.dot(diag_inverse[0], rhs[0], precision=highest, preferred_element_type=jnp.float32)
    update = jnp.dot(lower(0), first, precision=highest, preferred_element_type=jnp.float32).reshape(count, NB, NRHS)
    rhs = rhs - jnp.where((block_ids >= 1)[:, None, None], update, jnp.float32(0.0))
    second = jnp.dot(diag_inverse[1], rhs[1], precision=highest, preferred_element_type=jnp.float32)
    update = jnp.dot(lower(1), second, precision=highest, preferred_element_type=jnp.float32).reshape(count, NB, NRHS)
    rhs = rhs - jnp.where((block_ids >= 2)[:, None, None], update, jnp.float32(0.0))
    slots = jnp.arange(count, dtype=jnp.int32)
    block_of_slot = (slots % MB_DEV) * N_ROW + slots // MB_DEV
    trailing = jnp.take(rhs, block_of_slot, axis=0).reshape(count * NB, NRHS)
    return jnp.stack([first, second]), trailing
```

```python
import jax
import jax.numpy as jnp
from jax import lax
from jax.experimental import pallas as pl
from jax.experimental.pallas import tpu as pltpu
from jax.sharding import PartitionSpec as P

HIGHEST = lax.Precision.HIGHEST
HIGH = lax.Precision.HIGH
ANY = pl.BlockSpec(memory_space=pl.ANY)
SMEM = pl.BlockSpec(memory_space=pltpu.SMEM)


def ring(rows, shift):
    return [(i, (i + shift) % rows) for i in range(rows)]


def partners(rows, bit):
    return [(i, i ^ bit) for i in range(rows)]


def after(x, *events):
    return lax.optimization_barrier((x, *events))[0]


def mul(a, b, precision):
    return jnp.dot(a, b, precision=precision, preferred_element_type=jnp.float32)


def mul_t(a, b, precision):
    return lax.dot_general(
        a, b, (((0,), (0,)), ((), ())), precision=precision, preferred_element_type=jnp.float32
    )


def f32(*shape):
    return jax.ShapeDtypeStruct(shape, jnp.float32)


def opening(rows, first_shift, tiles, tile_block, panels, me):
    local, block, width = tiles.shape
    share = local // rows
    depth = panels.shape[1]
    half = block // 2
    chunks = block // width
    extra = depth * chunks // 2
    if chunks == 1:
        pieces = [[(0, h * extra, extra, 0)] for h in range(2)]
    else:
        pieces = [
            [(h * (chunks // 2) + k, 0, depth, k * depth) for k in range(chunks // 2)] for h in range(2)
        ]

    def kernel(block_ref, me_ref, tiles_ref, panels_ref, keep_ref, give_ref, sent_ref, order_ref, slots_ref, count, tile, halves, sem):
        me = me_ref[0]
        for shift in range(rows):
            count[shift] = 0

        def scan_mine(t, carry):
            shift = lax.rem(lax.rem(block_ref[me * local + t], rows) - me + rows, rows)
            seen = count[shift]
            order_ref[shift * share + seen] = t
            count[shift] = seen + 1
            return carry

        lax.fori_loop(0, local, scan_mine, 0)
        first_in = pltpu.make_async_copy(tiles_ref.at[order_ref[first_shift * share]], tile, sem.at[0])
        first_out = pltpu.make_async_copy(tile, sent_ref.at[0], sem.at[0])
        first_in.start()

        def find(t, carry):
            value = block_ref[t]
            return tuple(jnp.where(value == p, t, carry[p]) for p in range(2))

        at = lax.fori_loop(0, rows * local, find, (jnp.int32(0), jnp.int32(0)))
        bit0 = lax.rem(me, 2)

        def raw_in(p, k):
            start = pl.multiple_of((bit0 if k == 0 else 1 - bit0) * half, half)
            return pltpu.make_async_copy(
                tiles_ref.at[lax.rem(at[p], local), pl.ds(start, half)],
                halves.at[k, pl.ds(p * half, half)],
                sem.at[1 + 2 * p + k],
            )

        def corner_in(k, h):
            return [
                pltpu.make_async_copy(
                    panels_ref.at[0, pl.ds(start, size), pl.ds(chunk * width, width)],
                    halves.at[k, pl.ds(2 * half + to, size)],
                    sem.at[5 + k],
                )
                for chunk, start, size, to in pieces[h]
            ]

        for p in range(2):
            mine = at[p] // local == me

            @pl.when(mine)
            def _():
                for k in range(2):
                    raw_in(p, k).start()

            @pl.when(jnp.logical_not(mine))
            def _():
                for k in range(2):
                    halves[k, p * half : (p + 1) * half] = jnp.zeros((half, width), jnp.float32)

        for k in range(2):
            for h in range(2):

                @pl.when(jnp.logical_and(me == 1, bit0 == (h if k == 0 else 1 - h)))
                def _():
                    for copy in corner_in(k, h):
                        copy.start()

            @pl.when(me != 1)
            def _():
                halves[k, 2 * half :] = jnp.zeros((extra, width), jnp.float32)

        first_in.wait()
        first_out.start()
        for p in range(2):

            @pl.when(at[p] // local == me)
            def _():
                for k in range(2):
                    raw_in(p, k).wait()

        for k in range(2):

            @pl.when(me == 1)
            def _():
                for copy in corner_in(k, 0):
                    copy.wait()

        outs = [pltpu.make_async_copy(halves.at[k], ref, sem.at[1 + k]) for k, ref in enumerate((keep_ref, give_ref))]
        for copy in outs:
            copy.start()

        for shift in range(rows):
            source = lax.rem(me - shift + rows, rows)

            def scan_source(t, seen):
                value = block_ref[source * local + t]
                slots_ref[shift * share + seen] = value // rows
                return seen + (lax.rem(value, rows) == me).astype(jnp.int32)

            lax.fori_loop(0, local, scan_source, jnp.int32(0))
        first_out.wait()
        for copy in outs:
            copy.wait()

    return pl.pallas_call(
        kernel,
        out_shape=(
            f32(2 * half + extra, width),
            f32(2 * half + extra, width),
            f32(1, block, width),
            jax.ShapeDtypeStruct((local,), jnp.int32),
            jax.ShapeDtypeStruct((local + 8,), jnp.int32),
        ),
        in_specs=[SMEM, SMEM, ANY, ANY],
        out_specs=(ANY, ANY, ANY, SMEM, SMEM),
        scratch_shapes=[
            pltpu.SMEM((rows,), jnp.int32),
            pltpu.VMEM((block, width), jnp.float32),
            pltpu.VMEM((2, 2 * half + extra, width), jnp.float32),
            pltpu.SemaphoreType.DMA((7,)),
        ],
        cost_estimate=pl.CostEstimate(flops=0, bytes_accessed=6 << 20, transcendentals=0),
        name="opening",
    )(tile_block, me, tiles, panels)


def pack(plan, share, tiles, order):
    local, block, width = tiles.shape
    total = sum(hi - lo for _, lo, hi in plan)

    def kernel(order_ref, tiles_ref, *rest):
        sents, held, sem = rest[:-2], rest[-2], rest[-1]
        ins, outs = [], []
        for (shift, lo, hi), sent in zip(plan, sents):
            for c in range(lo, hi):
                n = len(ins)
                ins.append(
                    pltpu.make_async_copy(tiles_ref.at[order_ref[shift * share + c]], held.at[n], sem.at[n])
                )
                outs.append(pltpu.make_async_copy(held.at[n], sent.at[c - lo], sem.at[n]))
        for copy in ins:
            copy.start()
        for arrive, leave in zip(ins, outs):
            arrive.wait()
            leave.start()
        for copy in outs:
            copy.wait()

    return pl.pallas_call(
        kernel,
        out_shape=tuple(f32(hi - lo, block, width) for _, lo, hi in plan),
        in_specs=[SMEM, ANY],
        out_specs=tuple(ANY for _ in plan),
        scratch_shapes=[pltpu.VMEM((total, block, width), jnp.float32), pltpu.SemaphoreType.DMA((total,))],
        compiler_params=pltpu.CompilerParams(vmem_limit_bytes=32 << 20),
        cost_estimate=pl.CostEstimate(flops=0, bytes_accessed=8 * total * block * width, transcendentals=0),
        name="pack",
    )(order, tiles)


def settle(acc, source, slots, slot_at, count, order=None):
    local, block, width = acc.shape
    part = block // 2

    def kernel(slots_ref, order_ref, tile_ref, old_ref, new_ref):
        new_ref[...] = tile_ref[...] - old_ref[...]

    def at_tile(i, j, slots_ref, order_ref):
        return (i if order is None else order_ref[i], j, 0)

    def at_slot(i, j, slots_ref, order_ref):
        return (slots_ref[slot_at + i], j, 0)

    shape = (1, part, width)
    return pl.pallas_call(
        kernel,
        out_shape=jax.ShapeDtypeStruct(acc.shape, acc.dtype),
        grid_spec=pltpu.PrefetchScalarGridSpec(
            num_scalar_prefetch=2,
            grid=(count, block // part),
            in_specs=[pl.BlockSpec(shape, at_tile), pl.BlockSpec(shape, at_slot)],
            out_specs=pl.BlockSpec(shape, at_slot),
        ),
        input_output_aliases={3: 0},
        cost_estimate=pl.CostEstimate(flops=0, bytes_accessed=12 * count * block * width, transcendentals=0),
        name="settle",
    )(slots, slots if order is None else order, source, acc)


def shards(rhs_atlas, tile_block, panels, diag_inverse):
    rows = lax.axis_size("row")
    me = lax.axis_index("row").astype(jnp.int32)
    block = diag_inverse.shape[1]
    width = rhs_atlas.shape[1]
    local = rhs_atlas.shape[0] // block
    share = local // rows
    depth = panels.shape[1]
    half = block // 2
    tiles = rhs_atlas.reshape(local, block, width)

    keep, give, sent0, order, slots = opening(rows, 2, tiles, tile_block, panels, me[None])
    arrived = []

    def travel(part, sent, *events):
        if events:
            sent = after(sent, *events)
        got = lax.ppermute(sent, "row", ring(rows, part[0]))
        arrived.append((part, got))
        return got

    shifts = [2, 1] + list(range(3, rows))
    rounds = [[(2, 0, 1)], [(1, 0, 1)] + [(shift, 0, 1) for shift in shifts[2:]], [(shift, 1, 2) for shift in shifts]]
    last = [(shift, 2, share) for shift in shifts if share > 2]
    if last and share > 3:
        last[-1:] = [(rows - 1, 2, share - 1), (rows - 1, share - 1, share)]
    rounds.append(last)
    plan = sum(rounds[1:], [])
    sents = pack(plan, share, tiles, order)
    sent_of = dict(zip(plan, sents))
    sent_of[rounds[0][0]] = sent0

    def go(number, *events):
        return [travel(part, sent_of[part], *events) for part in rounds[number]]

    factor = lax.all_gather(panels, "col", axis=1, tiled=True)

    done = go(0)
    swap = lax.ppermute(give, "row", partners(rows, 1))
    keep = after(keep + swap, *done, *sents)
    done = go(1, keep)
    bit = 2
    while bit < rows:
        keep = keep + lax.ppermute(keep, "row", partners(rows, bit))
        bit *= 2
    keep = after(keep, *done)
    done = go(2, keep)
    other = lax.ppermute(keep, "row", partners(rows, 1))
    other = after(other, factor, *done)
    go(3, other)
    bit0 = me & 1
    low = jnp.where(bit0 == 0, keep, other)
    high = jnp.where(bit0 == 0, other, keep)
    raw = [jnp.concatenate([low[p * half : (p + 1) * half], high[p * half : (p + 1) * half]], axis=0) for p in range(2)]
    corner = jnp.concatenate([low[2 * half :], high[2 * half :]], axis=0)
    corner = corner.reshape(block // width, depth, width).transpose(1, 0, 2).reshape(depth, block)
    corner = lax.all_gather(corner, "col", axis=0, tiled=True)

    first = mul(diag_inverse[0], raw[0], HIGHEST)
    second = mul(diag_inverse[1], raw[1] - mul_t(corner, first, HIGHEST), HIGHEST)
    block_of_row = jnp.arange(local * block, dtype=jnp.int32)[:, None] // block * rows + me
    acc = jnp.where(block_of_row > 0, mul_t(factor[0], first, HIGH), 0.0)
    acc = acc + jnp.where(block_of_row > 1, mul_t(factor[1], second, HIGH), 0.0)
    acc = acc.reshape(local, block, width)

    acc = settle(acc, tiles, slots, 0, share, order)
    for (shift, lo, hi), got in arrived:
        acc = settle(acc, got, slots, shift * share + lo, hi - lo)
    return jnp.stack([first, second]), acc.reshape(local * block, width)


def solution(mesh):
    placed = (P("row", "col"), P(), P(None, "col", "row"), P())
    return jax.shard_map(
        shards,
        mesh=mesh,
        in_specs=placed,
        out_specs=(P(None, None, "col"), P("row", "col")),
        check_vma=False,
    )
```

```python
import jax
import jax.numpy as jnp
from jax import lax
from jax.experimental import pallas as pl
from jax.experimental.pallas import tpu as pltpu
from jax.sharding import PartitionSpec as P

HIGHEST = lax.Precision.HIGHEST
HIGH = lax.Precision.HIGH
ANY = pl.BlockSpec(memory_space=pl.ANY)
SMEM = pl.BlockSpec(memory_space=pltpu.SMEM)


def partners(rows, bits):
    return [(i, i ^ bits) for i in range(rows)]


def after(x, *events):
    return lax.optimization_barrier((x, *events))[0]


def mul(a, b, precision):
    return jnp.dot(a, b, precision=precision, preferred_element_type=jnp.float32)


def mul_t(a, b, precision):
    return lax.dot_general(
        a, b, (((0,), (0,)), ((), ())), precision=precision, preferred_element_type=jnp.float32
    )


def f32(*shape):
    return jax.ShapeDtypeStruct(shape, jnp.float32)


def opening(rows, tiles, tile_block, me):
    local, block, width = tiles.shape
    share = local // rows

    def kernel(block_ref, me_ref, tiles_ref, *rest):
        sent_refs, (order_ref, slots_ref, source_ref, count, held, sem) = rest[: rows + 1], rest[rows + 1 :]
        me = me_ref[0]
        for x in range(rows):
            count[x] = 0
        for early in (True, False):

            def scan_mine(t, carry):
                value = block_ref[me * local + t]
                x = lax.rem(value, rows) ^ me
                seen = count[x]
                hit = (value < 2) if early else (value >= 2)
                order_ref[jnp.where(hit, x * share + seen, local)] = t
                count[x] = seen + hit.astype(jnp.int32)
                return carry

            lax.fori_loop(0, local, scan_mine, 0)

        def find(t, carry):
            value = block_ref[t]
            return tuple(jnp.where(value == p, t, carry[p]) for p in range(2))

        ins, outs = [], []

        def move(tile, n):
            ins.append(pltpu.make_async_copy(tiles_ref.at[tile], held.at[n], sem.at[n]))
            outs.append(pltpu.make_async_copy(held.at[n], sent_refs[n].at[0], sem.at[n]))
            ins[-1].start()

        for x in range(1, rows):
            move(order_ref[x * share], x - 1)
        at = lax.fori_loop(0, rows * local, find, (jnp.int32(0), jnp.int32(0)))
        bit0 = lax.rem(me, 2)
        move(lax.rem(jnp.where(bit0 == 0, at[1], at[0]), local), rows - 1)
        move(lax.rem(jnp.where(bit0 == 0, at[0], at[1]), local), rows)
        for p in range(2):
            source_ref[p] = at[p] // local
        for x in range(rows):
            source = me ^ x
            seen = jnp.int32(0)
            for early in (True, False):

                def scan_source(t, seen):
                    value = block_ref[source * local + t]
                    hit = jnp.logical_and(lax.rem(value, rows) == me, (value < 2) if early else (value >= 2))
                    slots_ref[jnp.where(hit, x * share + seen, local)] = value // rows
                    return seen + hit.astype(jnp.int32)

                seen = lax.fori_loop(0, local, scan_source, seen)
        for arrive, leave in zip(ins, outs):
            arrive.wait()
            leave.start()
        for copy in outs:
            copy.wait()

    return pl.pallas_call(
        kernel,
        out_shape=tuple(f32(1, block, width) for _ in range(rows + 1))
        + tuple(jax.ShapeDtypeStruct((n,), jnp.int32) for n in (local + 8, local + 8, 8)),
        in_specs=[SMEM, SMEM, ANY],
        out_specs=(ANY,) * (rows + 1) + (SMEM,) * 3,
        scratch_shapes=[
            pltpu.SMEM((rows,), jnp.int32),
            pltpu.VMEM((rows + 1, block, width), jnp.float32),
            pltpu.SemaphoreType.DMA((rows + 1,)),
        ],
        compiler_params=pltpu.CompilerParams(vmem_limit_bytes=48 << 20),
        cost_estimate=pl.CostEstimate(flops=0, bytes_accessed=8 * (rows + 1) * block * width, transcendentals=0),
        name="opening",
    )(tile_block, me, tiles)


def pack(plan, share, tiles, order):
    local, block, width = tiles.shape
    total = sum(hi - lo for _, lo, hi in plan)

    def kernel(order_ref, tiles_ref, *rest):
        sents, held, sem = rest[:-2], rest[-2], rest[-1]
        ins, outs = [], []
        for (x, lo, hi), sent in zip(plan, sents):
            for c in range(lo, hi):
                n = len(ins)
                ins.append(pltpu.make_async_copy(tiles_ref.at[order_ref[x * share + c]], held.at[n], sem.at[n]))
                outs.append(pltpu.make_async_copy(held.at[n], sent.at[c - lo], sem.at[n]))
        for copy in ins:
            copy.start()
        for arrive, leave in zip(ins, outs):
            arrive.wait()
            leave.start()
        for copy in outs:
            copy.wait()

    return pl.pallas_call(
        kernel,
        out_shape=tuple(f32(hi - lo, block, width) for _, lo, hi in plan),
        in_specs=[SMEM, ANY],
        out_specs=tuple(ANY for _ in plan),
        scratch_shapes=[pltpu.VMEM((total, block, width), jnp.float32), pltpu.SemaphoreType.DMA((total,))],
        compiler_params=pltpu.CompilerParams(vmem_limit_bytes=48 << 20),
        cost_estimate=pl.CostEstimate(flops=0, bytes_accessed=8 * total * block * width, transcendentals=0),
        name="pack",
    )(order, tiles)


def settle(acc, source, slots, slot_at, count, order=None):
    local, block, width = acc.shape
    part = block // 2

    def kernel(slots_ref, order_ref, tile_ref, old_ref, new_ref):
        new_ref[...] = tile_ref[...] - old_ref[...]

    def at_tile(i, j, slots_ref, order_ref):
        return (i if order is None else order_ref[i], j, 0)

    def at_slot(i, j, slots_ref, order_ref):
        return (slots_ref[slot_at + i], j, 0)

    shape = (1, part, width)
    return pl.pallas_call(
        kernel,
        out_shape=jax.ShapeDtypeStruct(acc.shape, acc.dtype),
        grid_spec=pltpu.PrefetchScalarGridSpec(
            num_scalar_prefetch=2,
            grid=(count, block // part),
            in_specs=[pl.BlockSpec(shape, at_tile), pl.BlockSpec(shape, at_slot)],
            out_specs=pl.BlockSpec(shape, at_slot),
        ),
        input_output_aliases={3: 0},
        cost_estimate=pl.CostEstimate(flops=0, bytes_accessed=12 * count * block * width, transcendentals=0),
        name="settle",
    )(slots, slots if order is None else order, source, acc)


FINAL = [(1, 1, 4), (2, 2, 4), (3, 2, 3), (3, 3, 4)]


def exchange_of_four(me, panels, factor, firsts, spare, own, source, sent_of):
    block, width = own.shape[1:]
    bit0 = me % 2
    edges = partners(4, 1)
    arrived = []

    def travel(part, *events):
        sent = sent_of[part]
        if events:
            sent = after(sent, *events)
        got = lax.ppermute(sent, "row", partners(4, part[0]))
        arrived.append((part, got))
        return got

    corner = panels[0, :, :block]
    started = lax.dynamic_index_in_dim(source, bit0, 0, keepdims=False)

    corner_up = lax.ppermute(corner, "row", [(1, 3)])
    first = [None] + [travel((x, 0, 1)) for x in (1, 2, 3)]
    beside = lax.ppermute(spare, "row", [(2, 3), (3, 2)])
    away = started ^ me
    lower = jnp.where(away == 0, own, jnp.where(away == 1, first[1], jnp.where(away == 2, first[2], first[3])))
    lower = after(lower, beside, corner_up, *sent_of.values())

    second = travel((2, 1, 2), first[1], first[2], first[3], beside, corner_up)

    def upward(pairs):
        return lambda prime: lax.ppermute(prime, "row", pairs) if pairs else prime

    case = (source[0] < 2).astype(jnp.int32) + 2 * (source[1] < 2).astype(jnp.int32)
    up = lax.switch(case, [upward([]), upward([(0, 2)]), upward([(1, 3)]), upward([(0, 2), (1, 3)])], lower)
    upper = jnp.where(started == me, own, jnp.where(started == (me ^ 1), beside, up))
    prime = jnp.where(me < 2, lower, upper)
    corner = jnp.where(me < 2, corner, corner_up)

    parcel = jnp.concatenate([prime[0], corner.reshape(-1, width)], axis=0)
    parcel = after(parcel, second)
    third = travel((3, 1, 2), parcel)
    other = lax.ppermute(parcel, "row", edges)
    other = after(other, third, factor)

    for part in reversed(FINAL):
        travel(part, other)
    arrived = arrived[: -len(FINAL)] + arrived[: -len(FINAL) - 1 : -1]
    raw = [jnp.where(bit0 == p, parcel[:block], other[:block]) for p in range(2)]
    corner = jnp.where(bit0 == 1, parcel[block:], other[block:]).reshape(corner.shape)
    return raw, corner, arrived


def exchange(rows, me, panels, tiles, tile_block, sent_of):
    local, block, width = tiles.shape
    arrived = [(part, lax.ppermute(sent, "row", partners(rows, part[0]))) for part, sent in sent_of.items()]
    raw = []
    for p in range(2):
        at = jnp.argmax(tile_block == p)
        tile = lax.dynamic_index_in_dim(tiles, at % local, 0, keepdims=False)
        raw.append(lax.psum(jnp.where(at // local == me, tile, 0.0), "row"))
    corner = lax.psum(jnp.where(me == 1, panels[0, :, :block], 0.0), "row")
    return raw, corner, arrived


def shards(rhs_atlas, tile_block, panels, diag_inverse):
    rows = lax.axis_size("row")
    me = lax.axis_index("row").astype(jnp.int32)
    block = diag_inverse.shape[1]
    width = rhs_atlas.shape[1]
    local = rhs_atlas.shape[0] // block
    share = local // rows
    tiles = rhs_atlas.reshape(local, block, width)

    *firsts, spare, own, order, slots, source = opening(rows, tiles, tile_block, me[None])
    if rows == 4 and share == 4:
        plan = [(2, 1, 2), (3, 1, 2)] + FINAL
    else:
        plan = [(x, 1, share) for x in range(1, rows)]
    sent_of = dict(zip(plan, pack(plan, share, tiles, order)))
    sent_of.update({(x, 0, 1): sent for x, sent in zip(range(1, rows), firsts)})

    factor = lax.all_gather(panels, "col", axis=1, tiled=True)
    if rows == 4 and share == 4:
        raw, corner, arrived = exchange_of_four(me, panels, factor, firsts, spare, own, source, sent_of)
    else:
        raw, corner, arrived = exchange(rows, me, panels, tiles, tile_block, sent_of)
    corner = lax.all_gather(corner, "col", axis=0, tiled=True)

    first = mul(diag_inverse[0], raw[0], HIGHEST)
    second = mul(diag_inverse[1], raw[1] - mul_t(corner, first, HIGHEST), HIGHEST)
    block_of_row = jnp.arange(local * block, dtype=jnp.int32)[:, None] // block * rows + me
    acc = jnp.where(block_of_row > 0, mul_t(factor[0], first, HIGH), 0.0)
    acc = acc + jnp.where(block_of_row > 1, mul_t(factor[1], second, HIGH), 0.0)
    acc = acc.reshape(local, block, width)

    acc = settle(acc, tiles, slots, 0, share, order)
    for (x, lo, hi), got in arrived:
        acc = settle(acc, got, slots, x * share + lo, hi - lo)
    return jnp.stack([first, second]), acc.reshape(local * block, width)


def solution(mesh):
    placed = (P("row", "col"), P(), P(None, "col", "row"), P())
    return jax.shard_map(
        shards,
        mesh=mesh,
        in_specs=placed,
        out_specs=(P(None, None, "col"), P("row", "col")),
        check_vma=False,
    )
```

```python
import jax
import jax.numpy as jnp
from jax import lax
from jax.experimental import pallas as pl
from jax.experimental.pallas import tpu as pltpu
from jax.sharding import PartitionSpec as P

HIGHEST = lax.Precision.HIGHEST
HIGH = lax.Precision.HIGH
ANY = pl.BlockSpec(memory_space=pl.ANY)
SMEM = pl.BlockSpec(memory_space=pltpu.SMEM)


def partners(rows, bits):
    return [(i, i ^ bits) for i in range(rows)]


def after(x, *events):
    return lax.optimization_barrier((x, *events))[0]


def mul(a, b, precision):
    return jnp.dot(a, b, precision=precision, preferred_element_type=jnp.float32)


def mul_t(a, b, precision):
    return lax.dot_general(
        a, b, (((0,), (0,)), ((), ())), precision=precision, preferred_element_type=jnp.float32
    )


def f32(*shape):
    return jax.ShapeDtypeStruct(shape, jnp.float32)


def opening(rows, tiles, tile_block, me):
    local, block, width = tiles.shape
    share = local // rows

    def kernel(block_ref, me_ref, tiles_ref, *rest):
        sent_refs, (order_ref, source_ref, count, held, sem) = rest[:rows], rest[rows:]
        me = me_ref[0]
        for x in range(rows):
            count[x] = 0
        for t in range(local):
            value = block_ref[me * local + t]
            x = (value & (rows - 1)) ^ me
            seen = count[x]
            order_ref[x * share + jnp.where(value < 2, 0, share - 1 - seen)] = t
            count[x] = seen + (value >= 2).astype(jnp.int32)

        ins, outs = [], []

        def move(tile, n):
            ins.append(pltpu.make_async_copy(tiles_ref.at[tile], held.at[n], sem.at[n]))
            outs.append(pltpu.make_async_copy(held.at[n], sent_refs[n].at[0], sem.at[n]))
            ins[-1].start()

        for x in range(1, rows):
            move(order_ref[x * share], x - 1)
        at = [jnp.int32(0), jnp.int32(0)]
        for t in range(rows * local):
            value = block_ref[t]
            at = [jnp.where(value == p, t, at[p]) for p in range(2)]
        for p in range(2):
            source_ref[p] = at[p] // local
            source_ref[2 + p] = lax.rem(at[p], local)
        move(lax.rem(jnp.where((me & 1) == 0, at[1], at[0]), local), rows - 1)
        for arrive, leave in zip(ins, outs):
            arrive.wait()
            leave.start()
        for copy in outs:
            copy.wait()

    return pl.pallas_call(
        kernel,
        out_shape=tuple(f32(1, block, width) for _ in range(rows))
        + tuple(jax.ShapeDtypeStruct((n,), jnp.int32) for n in (local, 8)),
        in_specs=[SMEM, SMEM, ANY],
        out_specs=(ANY,) * rows + (SMEM,) * 2,
        scratch_shapes=[
            pltpu.SMEM((rows,), jnp.int32),
            pltpu.VMEM((rows, block, width), jnp.float32),
            pltpu.SemaphoreType.DMA((rows,)),
        ],
        compiler_params=pltpu.CompilerParams(vmem_limit_bytes=48 << 20),
        cost_estimate=pl.CostEstimate(flops=0, bytes_accessed=8 * rows * block * width, transcendentals=0),
        name="opening",
    )(tile_block, me, tiles)


def pack(plan, rows, tiles, tile_block, me, order, source):
    local, block, width = tiles.shape
    share = local // rows
    total = sum(hi - lo for _, lo, hi in plan)

    def kernel(block_ref, me_ref, order_ref, source_ref, tiles_ref, *rest):
        sents, (own_ref, slots_ref, held, sem) = rest[: len(plan)], rest[len(plan) :]
        me = me_ref[0]
        ins, outs = [], []

        def move(tile, to):
            n = len(ins)
            ins.append(pltpu.make_async_copy(tiles_ref.at[tile], held.at[n], sem.at[n]))
            outs.append(pltpu.make_async_copy(held.at[n], to, sem.at[n]))
            ins[-1].start()

        for (x, lo, hi), sent in zip(plan, sents):
            for c in range(lo, hi):
                move(order_ref[x * share + c], sent.at[c - lo])
        move(source_ref[2 + (me & 1)], own_ref.at[0])
        for arrive, leave in zip(ins, outs):
            arrive.wait()
            leave.start()
        for x in range(rows):
            first = (me ^ x) * local
            seen = jnp.int32(0)
            for t in range(local):
                value = block_ref[first + t]
                hit = (value & (rows - 1)) == me
                place = x * share + jnp.where(value < 2, 0, share - 1 - seen)
                slots_ref[jnp.where(hit, place, local)] = value // rows
                seen = seen + jnp.logical_and(hit, value >= 2).astype(jnp.int32)
        for copy in outs:
            copy.wait()

    *sents, own, slots = pl.pallas_call(
        kernel,
        out_shape=tuple(f32(hi - lo, block, width) for _, lo, hi in plan)
        + (f32(1, block, width), jax.ShapeDtypeStruct((local + 8,), jnp.int32)),
        in_specs=[SMEM, SMEM, SMEM, SMEM, ANY],
        out_specs=(ANY,) * (len(plan) + 1) + (SMEM,),
        scratch_shapes=[pltpu.VMEM((total + 1, block, width), jnp.float32), pltpu.SemaphoreType.DMA((total + 1,))],
        compiler_params=pltpu.CompilerParams(vmem_limit_bytes=48 << 20),
        cost_estimate=pl.CostEstimate(flops=0, bytes_accessed=8 * (total + 1) * block * width, transcendentals=0),
        name="pack",
    )(tile_block, me, order, source, tiles)
    return sents, own, slots


def settle(acc, source, slots, slot_at, count, order=None, parts=1):
    local, block, width = acc.shape
    part = block // parts

    def kernel(slots_ref, order_ref, tile_ref, old_ref, new_ref):
        new_ref[...] = tile_ref[...] - old_ref[...]

    def at_tile(i, j, slots_ref, order_ref):
        return (i if order is None else order_ref[i], j, 0)

    def at_slot(i, j, slots_ref, order_ref):
        return (slots_ref[slot_at + i], j, 0)

    shape = (1, part, width)
    return pl.pallas_call(
        kernel,
        out_shape=jax.ShapeDtypeStruct(acc.shape, acc.dtype),
        grid_spec=pltpu.PrefetchScalarGridSpec(
            num_scalar_prefetch=2,
            grid=(count, block // part),
            in_specs=[pl.BlockSpec(shape, at_tile), pl.BlockSpec(shape, at_slot)],
            out_specs=pl.BlockSpec(shape, at_slot),
        ),
        input_output_aliases={3: 0},
        cost_estimate=pl.CostEstimate(flops=0, bytes_accessed=12 * count * block * width, transcendentals=0),
        name="settle",
    )(slots, slots if order is None else order, source, acc)


FINAL = [(1, 1, 4), (2, 2, 4), (3, 2, 3), (3, 3, 4)]


def exchange_of_four(me, panels, factor, firsts, spare, own, source, sent_of):
    block, width = own.shape[1:]
    bit0 = me % 2
    edges = partners(4, 1)
    arrived = []

    def travel(part, *events):
        sent = sent_of[part]
        if events:
            sent = after(sent, *events)
        got = lax.ppermute(sent, "row", partners(4, part[0]))
        arrived.append((part, got))
        return got

    corner = panels[0, :, :block]
    started = lax.dynamic_index_in_dim(source, bit0, 0, keepdims=False)

    corner_up = lax.ppermute(corner, "row", [(1, 3)])
    first = [None] + [travel((x, 0, 1)) for x in (1, 2, 3)]
    beside = lax.ppermute(spare, "row", [(2, 3), (3, 2)])
    away = started ^ me
    lower = jnp.where(away == 0, own, jnp.where(away == 1, first[1], jnp.where(away == 2, first[2], first[3])))
    lower = after(lower, beside, corner_up, *sent_of.values())

    second = travel((2, 1, 2), first[1], first[2], first[3], beside, corner_up)

    def upward(pairs):
        return lambda prime: lax.ppermute(prime, "row", pairs) if pairs else prime

    case = (source[0] < 2).astype(jnp.int32) + 2 * (source[1] < 2).astype(jnp.int32)
    up = lax.switch(case, [upward([]), upward([(0, 2)]), upward([(1, 3)]), upward([(0, 2), (1, 3)])], lower)
    upper = jnp.where(started == me, own, jnp.where(started == (me ^ 1), beside, up))
    prime = jnp.where(me < 2, lower, upper)
    corner = jnp.where(me < 2, corner, corner_up)

    parcel = jnp.concatenate([prime[0], corner.reshape(-1, width)], axis=0)
    parcel = after(parcel, second)
    third = travel((3, 1, 2), parcel)
    other = lax.ppermute(parcel, "row", edges)
    other = after(other, factor)

    for part in reversed(FINAL):
        travel(part, other)
    arrived = arrived[: -len(FINAL)] + arrived[: -len(FINAL) - 1 : -1]
    other = after(other, third)
    raw = [jnp.where(bit0 == p, parcel[:block], other[:block]) for p in range(2)]
    corner = jnp.where(bit0 == 1, parcel[block:], other[block:]).reshape(corner.shape)
    return raw, corner, arrived


def exchange(rows, me, panels, tiles, tile_block, sent_of):
    local, block, width = tiles.shape
    arrived = [(part, lax.ppermute(sent, "row", partners(rows, part[0]))) for part, sent in sent_of.items()]
    raw = []
    for p in range(2):
        at = jnp.argmax(tile_block == p)
        tile = lax.dynamic_index_in_dim(tiles, at % local, 0, keepdims=False)
        raw.append(lax.psum(jnp.where(at // local == me, tile, 0.0), "row"))
    corner = lax.psum(jnp.where(me == 1, panels[0, :, :block], 0.0), "row")
    return raw, corner, arrived


def shards(rhs_atlas, tile_block, panels, diag_inverse):
    rows = lax.axis_size("row")
    me = lax.axis_index("row").astype(jnp.int32)
    block = diag_inverse.shape[1]
    width = rhs_atlas.shape[1]
    local = rhs_atlas.shape[0] // block
    share = local // rows
    tiles = rhs_atlas.reshape(local, block, width)

    *firsts, spare, order, source = opening(rows, tiles, tile_block, me[None])
    if rows == 4 and share == 4:
        plan = [(2, 1, 2), (3, 1, 2)] + FINAL
    else:
        plan = [(x, 1, share) for x in range(1, rows)]
    sents, own, slots = pack(plan, rows, tiles, tile_block, me[None], order, source)
    sent_of = dict(zip(plan, sents))
    sent_of.update({(x, 0, 1): sent for x, sent in zip(range(1, rows), firsts)})

    factor = lax.all_gather(panels, "col", axis=1, tiled=True)
    if rows == 4 and share == 4:
        raw, corner, arrived = exchange_of_four(me, panels, factor, firsts, spare, own, source, sent_of)
    else:
        raw, corner, arrived = exchange(rows, me, panels, tiles, tile_block, sent_of)
    corner = lax.all_gather(corner, "col", axis=0, tiled=True)

    first = mul(diag_inverse[0], raw[0], HIGHEST)
    second = mul(diag_inverse[1], raw[1] - mul_t(corner, first, HIGHEST), HIGHEST)
    block_of_row = jnp.arange(local * block, dtype=jnp.int32)[:, None] // block * rows + me
    acc = jnp.where(block_of_row > 0, mul_t(factor[0], first, HIGH), 0.0)
    acc = acc + jnp.where(block_of_row > 1, mul_t(factor[1], second, HIGH), 0.0)
    acc = acc.reshape(local, block, width)

    acc = settle(acc, tiles, slots, 0, share, order)
    for (x, lo, hi), got in arrived:
        acc = settle(acc, got, slots, x * share + lo, hi - lo)
    return jnp.stack([first, second]), acc.reshape(local * block, width)


def solution(mesh):
    placed = (P("row", "col"), P(), P(None, "col", "row"), P())
    return jax.shard_map(
        shards,
        mesh=mesh,
        in_specs=placed,
        out_specs=(P(None, None, "col"), P("row", "col")),
        check_vma=False,
    )
```
